128 devices in a mesh: seq: 8 (over x_hi, z), tp: 16 (over y, x_lo, core).
Axes of the slice: x: 4 (x_hi: 2, x_lo: 2; x = x_hi * 2 + x_lo), y: 4, z: 4, core: 2. Of those that a mesh axis runs over, the one named last changes fastest.
Arguments:
- teacher_hidden: bfloat16 [16384, 16384], P('seq', 'tp'), may hold values from -9 to 9
- teacher_gain: bfloat16 [16384], P('tp'), may hold values from 0.25 to 1.75
- target_proj: bfloat16 [16384, 4096], P('tp'), may hold values from -0.046875 to 0.046875
- student_in: bfloat16 [16384, 4096], P(('seq', 'tp')), may hold values from -6 to 6
- student_gain: bfloat16 [4096], replicated, may hold values from 0.25 to 1.75
- proj_weight: bfloat16 [4096, 4096], P('seq', 'tp'), may hold values from -0.09375 to 0.09375
- doc_ids: int32 [16384], P(('seq', 'tp')), may hold values from 0 to 63, never falling along the last dimension, each value on 1 to 1024 neighbouring positions
- stream_ids: int32 [16384], P(('seq', 'tp')), may hold values from 0 to 7
- stream_weight: float32 [8], replicated, may hold values from 0.25 to 4
Outputs:
- stream_loss: float32 [8], replicated
- w_grad: float32 [4096, 4096], P('seq', 'tp')
The draws below stay inside these ranges and needn't reach their ends.
Inputs may be any that keep to these rules, and one draw needn't show every extreme that they name: `doc_ids`: never falls along the tokens; every document holds 1 to 1024 tokens, and one holds exactly 1024.
All inputs are finite; a program needn't handle non-finite values.
Results may differ from the reference program's by a relative error of at most 0.02.
Values may be sent and summed in bfloat16 or wider, within the bound.
A program may use at most 128 MiB of HBM per device.

```python
import math
import jax
import jax.numpy as jnp
import numpy as np
from jax import lax

D = 4096
DT = 16384
NSTREAM = 8
TOKENS = 16384
DOCS = 64
DOC_MOST = 1024
N_TP = 16


def draw_teacher_hidden(key, part):
    key = jax.random.fold_in(key, 11)
    value_key = jax.random.fold_in(key, 1)
    position = jnp.arange(DT, dtype=jnp.float32) / (DT - 1)
    ramp = 0.5 * jnp.exp(jnp.log(6.0) * position)
    values = jnp.clip(jax.random.normal(value_key, (TOKENS, DT), jnp.float32), -3.0, 3.0)
    result = values * ramp[None, :]
    return result.astype(jnp.bfloat16)


def place_ends(drawn, stream_key, smallest, largest):
    dims = drawn.shape
    spot = [jax.random.randint(jax.random.fold_in(stream_key, axis), (), 0, dims[axis]) for axis in range(len(dims))]
    drawn = drawn.at[tuple(spot)].set(smallest)
    longest = dims.index(max(dims))
    spot[longest] = (spot[longest] + 1) % dims[longest]
    return drawn.at[tuple(spot)].set(largest)


def steps_of(rng, dims, cuts, low, largest):
    level, own = 1.0, jax.random.fold_in(rng, 6)
    for dim, parts in cuts:
        steps = jnp.exp(jax.random.uniform(jax.random.fold_in(own, dim), (parts,), jnp.float32, low / len(cuts), largest / len(cuts)))
        level = level * jnp.repeat(steps, dims[dim] // parts).reshape([-1 if axis == dim else 1 for axis in range(len(dims))])
    return level


def rank_bounds(number_of, slope):
    loads = [(1 << 20) // math.isqrt(grade ** slope) + 1 for grade in range(1, number_of + 1)]
    width = 1 + sum(loads) // (1 << 30)
    return np.cumsum(np.array([max(1, weight // width) for weight in loads]))


def skewed_ids(key, shape, amount, slope):
    listing = rank_bounds(amount, slope)
    ticket = jax.random.randint(jax.random.fold_in(key, 1), shape, 0, int(listing[amount - 1]))
    grade = jnp.searchsorted(jnp.asarray(listing, jnp.int32), ticket, side="right")
    return jax.random.permutation(jax.random.fold_in(key, 2), amount)[grade].astype(jnp.int32)


def profile(amount, total, limit, lean):
    weights = [(1 << 20) // math.isqrt(rank ** lean) + 1 for rank in range(2, amount + 1)]
    rest, holding = total - limit - (amount - 1), [1] * (amount - 1)
    while rest > 0:
        candidates = [i for i in range(amount - 1) if holding[i] < limit]
        mass, budget = sum([weights[i] for i in candidates]), rest
        for i in candidates:
            addition = min(limit - holding[i], max(1, budget * weights[i] // mass), rest)
            holding[i] = holding[i] + addition
            rest = rest - addition
    return np.array([limit] + holding)


def uneven_parts(rng, amount, total, limit, skew):
    if amount == 2:
        one = jax.random.randint(rng, (), max(1, total - limit), min(limit, total - 1) + 1)
        return jnp.stack([one, total - one])
    sizes = jnp.asarray(profile(amount, total, limit, skew), jnp.int32)
    couples = (amount - 1) // 2
    giver, taker = sizes[1:1 + 2 * couples:2], sizes[2:2 + 2 * couples:2]
    slack = jnp.minimum(giver - 1, limit - taker)
    shifted = jax.random.randint(jax.random.fold_in(rng, 1), (couples,), 0, 1 << 20) % (slack + 1)
    sizes = sizes.at[1:1 + 2 * couples:2].set(giver - shifted).at[2:2 + 2 * couples:2].set(taker + shifted)
    return sizes[jax.random.permutation(jax.random.fold_in(rng, 2), amount)]


def normal_values(own_key, shape, scale, most, split=(), kind=jnp.bfloat16):
    factor_of = steps_of(own_key, shape, split, -0.22, 0.18) if split else 1.0
    array = jax.random.normal(own_key, shape, jnp.float32) * scale * factor_of
    return jnp.minimum(jnp.maximum(array, -most), most).astype(kind)


def setup_inputs(seed: int = 0) -> dict:
    streams_of = jax.random.split(jax.random.key(seed), 10)
    teacher_hidden = draw_teacher_hidden(jax.random.fold_in(streams_of[9], 71), 0)
    teacher_gain = jnp.clip(1.0 + 0.15 * jax.random.normal(streams_of[1], (DT,), jnp.float32), 0.25, 1.75).astype(jnp.bfloat16)
    target_proj = normal_values(streams_of[2], (DT, D), DT ** -0.5, 0.046875, ((0, 16),))
    student_in = normal_values(streams_of[3], (TOKENS, D), 1.0, 6.0, ((0, 128),))
    student_gain = jnp.clip(1.0 + 0.15 * jax.random.normal(streams_of[4], (D,), jnp.float32), 0.25, 1.75).astype(jnp.bfloat16)
    proj_weight = normal_values(streams_of[5], (D, D), D ** -0.5, 0.09375, ((0, 8), (1, 16)))
    doc_ids = jnp.searchsorted(jnp.cumsum(uneven_parts(streams_of[6], DOCS, TOKENS, DOC_MOST, 2)), jnp.arange(TOKENS), side="right").astype(jnp.int32)
    stream_ids = place_ends(skewed_ids(streams_of[7], (TOKENS,), NSTREAM, 2), jax.random.fold_in(streams_of[7], 3), 0, NSTREAM - 1).astype(jnp.int32)
    stream_weight = jnp.clip(jnp.exp(jax.random.uniform(streams_of[8], (NSTREAM,), jnp.float32, math.log(0.25), math.log(4.0))), 0.25, 4.0)
    return dict(teacher_hidden=teacher_hidden, teacher_gain=teacher_gain, target_proj=target_proj, student_in=student_in, student_gain=student_gain, proj_weight=proj_weight, doc_ids=doc_ids, stream_ids=stream_ids, stream_weight=stream_weight)


EPS = 1e-05

def reference(teacher_hidden, teacher_gain, target_proj, student_in, student_gain, proj_weight, doc_ids, stream_ids, stream_weight):
    teacher_float = teacher_hidden.astype(jnp.float32)
    teacher_mean = lax.optimization_barrier(jnp.mean(teacher_float * teacher_float, axis=1, keepdims=True))
    teacher_normed = (teacher_float * lax.rsqrt(teacher_mean + EPS) * teacher_gain.astype(jnp.float32)[None, :]).astype(jnp.bfloat16)
    block_width = DT // N_TP
    target = jnp.zeros((TOKENS, D), jnp.float32)
    for block_index in range(N_TP):
        lower = block_index * block_width
        partial_sum = jnp.dot(teacher_normed[:, lower:lower + block_width], target_proj[lower:lower + block_width], preferred_element_type=jnp.float32)
        target = target + lax.optimization_barrier(partial_sum.astype(jnp.bfloat16)).astype(jnp.float32)
    student_float = student_in.astype(jnp.float32)
    student_mean = lax.optimization_barrier(jnp.mean(student_float * student_float, axis=1, keepdims=True))
    normed = (student_float * lax.rsqrt(student_mean + EPS) * student_gain.astype(jnp.float32)[None, :]).astype(jnp.bfloat16)
    hidden = jnp.dot(normed, proj_weight, preferred_element_type=jnp.float32).astype(jnp.bfloat16)
    error = student_float + hidden.astype(jnp.float32) - target
    doc_count = jnp.zeros((DOCS,), jnp.float32).at[doc_ids].add(1.0)
    doc_length = doc_count[doc_ids]
    token_error = lax.optimization_barrier(jnp.mean(error * error, axis=1))
    stream_table = (stream_ids[:, None] == jnp.arange(NSTREAM, dtype=jnp.int32)[None, :]).astype(jnp.float32)
    stream_loss = lax.optimization_barrier(jnp.sum(stream_table * (token_error / doc_length)[:, None], axis=0))
    scale = 2.0 * stream_weight[stream_ids] / doc_length
    grad_rows = (scale[:, None] * error).astype(jnp.bfloat16)
    w_grad = jnp.dot(normed.T, grad_rows, preferred_element_type=jnp.float32)
    return (stream_loss, w_grad)
```

```python
import jax
import jax.numpy as jnp
from jax import lax
from jax.experimental import pallas as pl
from jax.experimental.pallas import tpu as pltpu
from jax.sharding import PartitionSpec as P

EPS = 1e-05
DT = 16384
D = 4096
NC = 4
SLOTS = 3
BF = jnp.bfloat16
F32 = jnp.float32
MESH = pl.DeviceIdType.MESH


def device(xh, z, y, xl, c):
    return {"seq": xh * 4 + z, "tp": (y * 2 + xl) * 2 + c}


def kernel(
    teacher,
    tgain,
    proj,
    student,
    sgain,
    weight,
    meta,
    wvec,
    out_t,
    out_loss,
    a_buf,
    b_buf,
    p_buf,
    r1_buf,
    r2_buf,
    sx_buf,
    rx_buf,
    nd_buf,
    w_buf,
    hs_buf,
    hr_buf,
    st_buf,
    gs_buf,
    gr_buf,
    gt_buf,
    dr1_buf,
    dr2_buf,
    ds_buf,
    dy_buf,
    fs_buf,
    fr_buf,
    m_buf,
    sq_buf,
    stat_buf,
    statr_buf,
    staty_buf,
    statz_buf,
    stato_buf,
    loss_buf,
    lossr_buf,
    rs_buf,
    sc_buf,
    ln_buf,
    te_buf,
    own_buf,
    send_sem,
    recv_sem,
    local_sem,
    cross_sem,
):
    s = lax.axis_index("seq")
    t = lax.axis_index("tp")
    xh, z = s // 4, s % 4
    y, xl, c = t // 4, (t // 2) % 2, t % 2
    x = xh * 2 + xl
    o = 1 - c

    def at_y(k):
        return device(xh, z, (y + k) % 4, xl, c)

    def at_z(k):
        return device(xh, (z + k) % 4, y, xl, c)

    def at_x(k):
        n = (x + k) % 4
        return device(n // 2, z, y, n % 2, c)

    sibling = device(xh, z, y, xl, o)
    x_pair = device(xh, z, y, 1 - xl, c)
    x_outer = device(1 - xh, z, y, 1 - xl, c)

    counts = {"s": 0, "r": 0, "l": 0}
    pending = []

    def local(src, dst):
        i = counts["l"]
        counts["l"] += 1
        cp = pltpu.make_async_copy(src, dst, local_sem.at[i])
        cp.start()
        return cp

    def remote(src, dst, to):
        i = counts["s"]
        counts["s"] += 1
        cp = pltpu.make_async_remote_copy(
            src_ref=src,
            dst_ref=dst,
            send_sem=send_sem.at[i],
            recv_sem=recv_sem.at[i],
            device_id=to,
            device_id_type=MESH,
        )
        cp.start()
        pending.append(cp)
        return cp

    def sent(cps):
        for cp in cps:
            cp.wait_send()
            pending[:] = [other for other in pending if other is not cp]

    def crossed(src, dst, to, itself, base):
        i = counts["s"]
        counts["s"] += 1
        cp = pltpu.make_async_remote_copy(
            src_ref=src,
            dst_ref=dst,
            send_sem=send_sem.at[i],
            recv_sem=cross_sem.at[base + xl],
            device_id=to,
            device_id_type=MESH,
        )
        own = pltpu.make_async_copy(src, dst, cross_sem.at[base + xl])

        @pl.when(itself)
        def _():
            own.start()

        @pl.when(jnp.logical_not(itself))
        def _():
            cp.start()

        return cp, itself

    def crossed_sent(pair):
        cp, itself = pair

        @pl.when(jnp.logical_not(itself))
        def _():
            cp.wait_send()

    st_load = local(student, st_buf.at[c])
    order = [2, 1, 3, 0]
    blocks = [((y + k) % 4) * 2 + h for k in order for h in range(2)]
    a_load = [local(teacher.at[b], a_buf.at[c, b]) for b in blocks]
    m_load = local(meta, m_buf.at[c])

    def proj_cols(j, yp, core):
        lane = yp * 1024 + (j // 2) * 512 + (j % 2) * 128 + core * 256
        return proj.at[:, :, pl.ds(pl.multiple_of(lane, 128), 128)]

    b_load = [
        [local(proj_cols(j, yp, c), b_buf.at[c, j, :, :, pl.ds(yp * 128, 128)]) for yp in range(4)]
        for j in range(NC)
    ]

    swapped = [device(xh, y, z, r, c) for r in range(2)]
    barrier = pltpu.get_barrier_semaphore()
    peers = [sibling, at_x(1), at_x(3)] + [at_y(k) for k in (1, 2, 3)] + [at_z(k) for k in (1, 2, 3)]
    for peer in peers:
        pl.semaphore_signal(barrier, inc=1, device_id=peer, device_id_type=MESH)

    @pl.when(y != z)
    def _():
        for peer in swapped:
            pl.semaphore_signal(barrier, inc=1, device_id=peer, device_id_type=MESH)
        pl.semaphore_wait(barrier, len(peers) + 2)

    @pl.when(y == z)
    def _():
        pl.semaphore_wait(barrier, len(peers))

    w_swap = [
        crossed(
            weight.at[pl.ds(r * 256, 256)],
            w_buf.at[xh * 2 + r, z, :, pl.ds(pl.multiple_of(xl * 256, 128), 256)],
            swapped[r],
            jnp.logical_and(y == z, xl == r),
            0,
        )
        for r in range(2)
    ]

    def send_b(j):
        return [
            remote(proj_cols(j, yp, o), b_buf.at[c, j, :, :, pl.ds(yp * 128, 128)], sibling)
            for yp in range(4)
        ]

    b_recv = [send_b(0)]

    st_load.wait()
    sgain_f = sgain[...].astype(F32)

    def norm_rows(i, _):
        rows = pl.ds(pl.multiple_of(i * 16, 16), 16)
        v = st_buf[c, rows, :].astype(F32)
        scale = lax.rsqrt(jnp.sum(v * v, axis=1, keepdims=True) / D + EPS)
        n = (v * scale * sgain_f).astype(BF)
        for p in range(4):
            for zp in range(4):
                src = (p // 2) * 2048 + zp * 512 + (p % 2) * 256
                nd_buf[z, c, rows, pl.ds(p * 1024 + zp * 256, 256)] = n[:, src : src + 256]
        return 0

    lax.fori_loop(0, 8, norm_rows, 0)

    def half(h):
        return pl.ds(h * 64, 64)

    nd_right, nd_left = [None, None], [None, None]
    for first in range(2):
        h = first
        nd_right[h] = remote(nd_buf.at[z, c, half(h)], nd_buf.at[z, c, half(h)], at_z(1))
        h = 1 - first
        nd_left[h] = remote(nd_buf.at[z, c, half(h)], nd_buf.at[z, c, half(h)], at_z(3))

    tgain_f = tgain[...].astype(F32)
    ones = jnp.ones((8, 1024), BF)
    a_recv = []
    for load, b in zip(a_load, blocks):
        load.wait()

        def prep(r, _, b=b):
            rows = pl.ds(pl.multiple_of(r * 128, 128), 128)
            v = a_buf[c, b, rows, :].astype(F32)
            squares = (v * v).astype(BF)
            sq_buf[b * 2 + r] = lax.dot_general(
                ones, squares, (((1,), (1,)), ((), ())), preferred_element_type=F32
            )
            a_buf[c, b, rows, :] = (v * tgain_f).astype(BF)
            return 0

        lax.fori_loop(0, 2, prep, 0)
        a_recv.append(remote(a_buf.at[c, b], a_buf.at[c, b], sibling))

    st_recv = remote(st_buf.at[c], st_buf.at[c], sibling)
    m_load.wait()
    m_recv = remote(m_buf.at[c], m_buf.at[c], sibling)
    nd_side = [remote(nd_buf.at[z, c], nd_buf.at[z, c], sibling)]
    for j in range(1, NC):
        b_recv.append(send_b(j))

    for n in range(2):
        got = w_buf.at[x, y, :, pl.ds(n * 256, 256)]
        pltpu.make_async_copy(got, got, cross_sem.at[n]).wait()

    def cols(h):
        return pl.ds(h * 256, 256)

    w_y = [
        [remote(w_buf.at[x, y, :, cols(h)], w_buf.at[x, y, :, cols(h)], at_y(k)) for k in (1, 2, 3)]
        for h in range(2)
    ]

    for i in range(16):
        stat_buf[0, i : i + 1, :] = sq_buf[i, 0:1, :]
    own_counts = jnp.sum(m_buf[c], axis=0, keepdims=True)
    stat_buf[0, 16:24, :] = jnp.broadcast_to(own_counts, (8, 128))

    stat_c = remote(stat_buf.at[0], statr_buf.at[0], sibling)

    def block_out(j, k):
        slot = j % SLOTS

        def body(h, _):
            b = ((y + k) % 4) * 2 + h
            acc = jnp.dot(
                a_buf[0, b], b_buf[0, j].reshape(1024, 512), preferred_element_type=F32
            )
            acc = acc + jnp.dot(
                a_buf[1, b], b_buf[1, j].reshape(1024, 512), preferred_element_type=F32
            )
            p_buf[slot, b] = acc.astype(BF)
            return 0

        lax.fori_loop(0, 2, body, 0)

    r1 = [None] * NC
    r2 = [None] * NC
    p_sends = [None] * NC

    def part(k, h):
        return ((y + k) % 4) * 2 + h

    def stage_a(j):
        slot = j % SLOTS
        if j >= SLOTS:
            sent(p_sends[j - SLOTS])
        for cp in b_load[j]:
            cp.wait()
        for cp in b_recv[j]:
            cp.wait_recv()
        for n, k in enumerate(order):
            if j == 0:
                a_recv[2 * n].wait_recv()
                a_recv[2 * n + 1].wait_recv()
            block_out(j, k)
            if k == 2:
                r1[j] = [
                    remote(p_buf.at[slot, part(2, 0)], r1_buf.at[j, 0], at_y(1)),
                    remote(p_buf.at[slot, part(2, 1)], r1_buf.at[j, 1], at_y(3)),
                ]
            elif k == 1:
                right = remote(p_buf.at[slot, part(1, 1)], r2_buf.at[j, 0, 1], at_y(1))
            elif k == 3:
                left = remote(p_buf.at[slot, part(3, 0)], r2_buf.at[j, 1, 0], at_y(3))
        r2[j] = [right, left]
        p_sends[j] = r1[j] + [right, left]

    def stage_b(j):
        slot = j % SLOTS
        for i, (k, h) in enumerate(((1, 0), (3, 1))):
            r1[j][i].wait_recv()
            b = part(k, h)
            p_buf[slot, b] = (p_buf[slot, b].astype(F32) + r1_buf[j, i].astype(F32)).astype(BF)
            cp = remote(p_buf.at[slot, b], r2_buf.at[j, i, h], at_y(k))
            r2[j].append(cp)
            p_sends[j].append(cp)

    def summed(j, h, lanes):
        slot = j % SLOTS
        return (
            p_buf[slot, part(0, h), :, lanes].astype(F32)
            + r2_buf[j, 0, h, :, lanes].astype(F32)
            + r2_buf[j, 1, h, :, lanes].astype(F32)
        )

    rx = [None] * NC

    def stage_c(j):
        for cp in r2[j]:
            cp.wait_recv()
        for i in range(4):
            lanes = pl.ds(i * 128, 128)
            sx_buf[j, :, lanes] = summed(j, 1 - xl, lanes).astype(BF)
            own_buf[j % 2, :, lanes] = summed(j, xl, lanes)
        rx[j] = remote(sx_buf.at[j], rx_buf.at[j], x_pair)

    gr = [None] * NC

    def stage_d(j):
        rx[j].wait_recv()
        for yp in range(4):
            lanes = pl.ds(yp * 128, 128)
            target = own_buf[j % 2, :, lanes] + rx_buf[j, :, lanes].astype(F32)
            lane = yp * 1024 + (j // 2) * 512 + (j % 2) * 128 + c * 256
            st = st_buf[:, :, pl.ds(pl.multiple_of(lane, 128), 128)].reshape(256, 128)
            hidden = hr_buf[yp, :, pl.ds(j * 128, 128)]
            error = st.astype(F32) + hidden.astype(F32) - target * rs_buf[...]
            if j == 0 and yp == 0:
                te_buf[...] = error * error
            else:
                te_buf[...] += error * error
            gs_buf[j, yp] = (error * sc_buf[...]).astype(BF)
        gr[j] = [
            remote(gs_buf.at[j, (z + k) % 4], gr_buf.at[j, z], at_z(k)) for k in (2, 1, 3)
        ]
        gr_buf[j, z] = gs_buf[j, z]

    d1 = [None] * NC
    d2 = [None] * NC

    def dpart(k, h):
        return ((x + k) % 4) * 2 + h

    def stage_e(j):
        for cp in gr[j]:
            cp.wait_recv()
        gt_buf[...] = gr_buf[j].reshape(1024, 128).T
        for k in order:

            def body(h, _, k=k):
                b = dpart(k, h)
                lanes = pl.ds(pl.multiple_of(b * 512, 512), 512)
                nd = nd_buf[:, :, :, lanes].reshape(1024, 512)
                b_buf[0, j, b] = jnp.dot(gt_buf[...], nd, preferred_element_type=F32).astype(BF)
                return 0

            lax.fori_loop(0, 2, body, 0)
            if k == 2:
                d1[j] = [
                    remote(b_buf.at[0, j, dpart(2, 0)], dr1_buf.at[j, 0], at_x(1)),
                    remote(b_buf.at[0, j, dpart(2, 1)], dr1_buf.at[j, 1], at_x(3)),
                ]
            elif k == 1:
                right = remote(b_buf.at[0, j, dpart(1, 1)], dr2_buf.at[j, 0, 1], at_x(1))
            elif k == 3:
                left = remote(b_buf.at[0, j, dpart(3, 0)], dr2_buf.at[j, 1, 0], at_x(3))
        d2[j] = [right, left]

    def stage_f(j):
        for i, (k, h) in enumerate(((1, 0), (3, 1))):
            d1[j][i].wait_recv()
            b = dpart(k, h)
            b_buf[0, j, b] = (b_buf[0, j, b].astype(F32) + dr1_buf[j, i].astype(F32)).astype(BF)
            d2[j].append(remote(b_buf.at[0, j, b], dr2_buf.at[j, i, h], at_x(k)))

    dy = [None] * NC

    def stage_g(j):
        for cp in d2[j]:
            cp.wait_recv()
        for zp in range(4):
            h, lanes = zp // 2, pl.ds((zp % 2) * 256, 256)
            ds_buf[j, zp] = (
                b_buf[0, j, dpart(0, h), :, lanes].astype(F32)
                + dr2_buf[j, 0, h, :, lanes].astype(F32)
                + dr2_buf[j, 1, h, :, lanes].astype(F32)
            ).astype(BF)
        dy[j] = [
            remote(ds_buf.at[j, (y + k) % 4], dy_buf.at[j, y], at_y(k)) for k in (2, 1, 3)
        ]

    final = [None] * NC

    def stage_h(j):
        for cp in dy[j]:
            cp.wait_recv()
        total = ds_buf[j, y].astype(F32)
        for k in (1, 2, 3):
            total = total + dy_buf[j, (y + k) % 4].astype(F32)
        fs_buf[j] = total.astype(BF)
        final[j] = crossed(
            fs_buf.at[j],
            fr_buf.at[j % 2, xl],
            device(xh, y, z, j // 2, c),
            jnp.logical_and(y == z, xl == j // 2),
            2 + 2 * (j % 2),
        )

    w_x = [None, None]

    def gather_x1(h):
        for cp in w_y[h]:
            cp.wait_recv()
        w_x[h] = [remote(w_buf.at[x, :, :, cols(h)], w_buf.at[x, :, :, cols(h)], at_x(k)) for k in (1, 3)]

    w_f = [None, None]

    def gather_x2(h):
        w_x[h][0].wait_recv()
        left = w_buf.at[(x + 3) % 4, pl.ds(0, 2), :, cols(h)]
        a = remote(left, left, at_x(1))
        w_x[h][1].wait_recv()
        right = w_buf.at[(x + 1) % 4, pl.ds(2, 2), :, cols(h)]
        w_f[h] = [a, remote(right, right, at_x(3))]

    stage_a(0)
    stat_c.wait_recv()
    stat_buf[1] = stat_buf[0] + statr_buf[0]
    stat_x = remote(stat_buf.at[1], statr_buf.at[1], x_pair)
    gather_x1(0)
    stage_a(1)

    nd_right[0].wait_recv()
    from_left = nd_buf.at[(z + 3) % 4, c, half(0)]
    nd_f0 = remote(from_left, from_left, at_z(1))
    nd_left[1].wait_recv()
    from_right = nd_buf.at[(z + 1) % 4, c, half(1)]
    nd_f1 = remote(from_right, from_right, at_z(3))
    gather_x1(1)
    stat_x.wait_recv()
    stat_buf[2] = stat_buf[1] + statr_buf[1]
    stat_y = [remote(stat_buf.at[2], staty_buf.at[y], at_y(k)) for k in (1, 2, 3)]
    staty_buf[y] = stat_buf[2]

    stage_b(0)
    stage_a(2)
    gather_x2(0)
    for cp in stat_y:
        cp.wait_recv()
    stat = staty_buf[0] + staty_buf[1] + staty_buf[2] + staty_buf[3]
    stat_buf[3] = stat
    statz_buf[z] = stat[16:24]
    stat_z = [remote(stat_buf.at[3, pl.ds(16, 8)], statz_buf.at[z], at_z(k)) for k in (1, 2, 3)]
    nd_right[1].wait_recv()
    nd_left[0].wait_recv()
    for k in (1, 3):
        whole = nd_buf.at[(z + k) % 4, c]
        nd_side.append(remote(whole, whole, sibling))
    stage_b(1)
    gather_x2(1)
    for cp in stat_z:
        cp.wait_recv()
    stato_buf[0] = statz_buf[0] + statz_buf[1] + statz_buf[2] + statz_buf[3]
    stat_o = remote(stato_buf.at[0], stato_buf.at[1], x_outer)
    nd_f0.wait_recv()
    nd_f1.wait_recv()
    whole = nd_buf.at[(z + 2) % 4, c]
    nd_side.append(remote(whole, whole, sibling))
    stage_c(0)
    stage_a(3)

    stat_o.wait_recv()
    m_recv.wait_recv()
    lanes_i = lax.broadcasted_iota(jnp.int32, (8, 128), 1)
    doc_counts = jnp.where(lanes_i < 64, stato_buf[0] + stato_buf[1], 0.0)[0:1]
    stream_w = wvec[0:1]
    rows_i = lax.broadcasted_iota(jnp.int32, (24, 128), 0)
    eye = lax.broadcasted_iota(jnp.int32, (128, 128), 0) == lax.broadcasted_iota(
        jnp.int32, (128, 128), 1
    )
    for core in range(2):
        rows = pl.ds(core * 128, 128)
        row = jnp.sum(
            jnp.where(rows_i == (y * 2 + xl) * 2 + core, stat_buf[3], 0.0), axis=0, keepdims=True
        )
        col = jnp.sum(
            jnp.where(eye, jnp.broadcast_to(row, (128, 128)), 0.0), axis=1, keepdims=True
        )
        rs_buf[rows] = jnp.broadcast_to(lax.rsqrt(col / DT + EPS), (128, 128))
        m = m_buf[core]
        length = jnp.sum(m * doc_counts, axis=1, keepdims=True)
        sw = jnp.sum(m * stream_w, axis=1, keepdims=True)
        sc_buf[rows] = jnp.broadcast_to(2.0 * sw / length, (128, 128))
        ln_buf[rows] = jnp.broadcast_to(length, (128, 128))
    st_recv.wait_recv()

    for cp in nd_side:
        cp.wait_recv()
    for h in range(2):
        for cp in w_f[h]:
            cp.wait_recv()
    hr = []
    for k in order:
        zd = (z + k) % 4
        hs_buf[zd] = jnp.dot(
            nd_buf[zd].reshape(256, D), w_buf[...].reshape(D, 512), preferred_element_type=F32
        ).astype(BF)
        if k:
            hr.append(remote(hs_buf.at[zd], hr_buf.at[z], at_z(k)))
    hr_buf[z] = hs_buf[z]

    stage_b(2)
    stage_c(1)
    for cp in hr:
        cp.wait_recv()
    stage_d(0)
    stage_d(1)
    stage_b(3)
    stage_e(0)
    stage_c(2)
    stage_f(0)
    stage_e(1)
    stage_d(2)
    stage_g(0)
    stage_f(1)
    stage_e(2)
    stage_h(0)
    stage_c(3)
    stage_g(1)
    stage_f(2)
    stage_d(3)

    def loss_of(core):
        rows = pl.ds(core * 128, 128)
        te = jnp.sum(te_buf[rows], axis=1, keepdims=True) / D
        return jnp.sum(m_buf[core] * (te / ln_buf[rows]), axis=0, keepdims=True)

    loss_buf[0] = jnp.broadcast_to(loss_of(0) + loss_of(1), (8, 128))
    loss_c = remote(loss_buf.at[0], lossr_buf.at[0], sibling)
    stage_h(1)
    stage_e(3)
    loss_c.wait_recv()
    loss_buf[1] = loss_buf[0] + lossr_buf[0]
    loss_x = remote(loss_buf.at[1], lossr_buf.at[1], x_pair)
    stage_g(2)
    stage_f(3)
    loss_x.wait_recv()
    loss_buf[2] = loss_buf[1] + lossr_buf[1]
    lossr_buf[4 + y] = loss_buf[2]
    loss_y = [remote(loss_buf.at[2], lossr_buf.at[4 + y], at_y(k)) for k in (1, 2, 3)]
    stage_h(2)
    for cp in loss_y:
        cp.wait_recv()
    loss_buf[3] = lossr_buf[4] + lossr_buf[5] + lossr_buf[6] + lossr_buf[7]
    lossr_buf[8 + z] = loss_buf[3]
    loss_z = [remote(loss_buf.at[3], lossr_buf.at[8 + z], at_z(k)) for k in (1, 2, 3)]
    stage_g(3)
    for cp in loss_z:
        cp.wait_recv()
    loss_buf[4] = lossr_buf[8] + lossr_buf[9] + lossr_buf[10] + lossr_buf[11]
    loss_o = remote(loss_buf.at[4], lossr_buf.at[2], x_outer)
    stage_h(3)
    loss_o.wait_recv()
    out_loss[...] = loss_buf[4] + lossr_buf[2]

    for jj in range(2):
        for r in range(2):
            got = fr_buf.at[jj, r]
            pltpu.make_async_copy(got, got, cross_sem.at[2 + 2 * jj + r]).wait()
    for pair in w_swap + final:
        crossed_sent(pair)
    for jj in range(2):
        for r in range(2):
            out_t[pl.ds(jj * 128, 128), pl.ds(r * 256, 256)] = fr_buf[jj, r]
    for cp in list(pending):
        cp.wait_send()


def shards(
    teacher_hidden,
    teacher_gain,
    target_proj,
    student_in,
    student_gain,
    proj_weight,
    doc_ids,
    stream_ids,
    stream_weight,
):
    lane = jnp.arange(128, dtype=jnp.int32)[None, :]
    meta = jnp.where(
        lane < 64, doc_ids[:, None] == lane, stream_ids[:, None] == lane - 64
    ).astype(F32)
    wvec = jnp.broadcast_to(jnp.pad(stream_weight, (64, 56))[None, :], (8, 128))
    hbm = pl.BlockSpec(memory_space=pl.ANY)
    vmem = pl.BlockSpec(memory_space=pltpu.VMEM)
    scratch = [
        ((2, 8, 256, 1024), BF),
        ((2, NC, 8, 128, 512), BF),
        ((SLOTS, 8, 256, 512), BF),
        ((NC, 2, 256, 512), BF),
        ((NC, 2, 2, 256, 512), BF),
        ((NC, 256, 512), BF),
        ((NC, 256, 512), BF),
        ((4, 2, 128, D), BF),
        ((4, 4, 256, 512), BF),
        ((4, 256, 512), BF),
        ((4, 256, 512), BF),
        ((2, 128, D), BF),
        ((NC, 4, 256, 128), BF),
        ((NC, 4, 256, 128), BF),
        ((128, 1024), BF),
        ((NC, 2, 128, 512), BF),
        ((NC, 2, 2, 128, 512), BF),
        ((NC, 4, 128, 256), BF),
        ((NC, 4, 128, 256), BF),
        ((NC, 128, 256), BF),
        ((2, 2, 128, 256), BF),
        ((2, 128, 128), F32),
        ((16, 8, 128), F32),
        ((4, 24, 128), F32),
        ((2, 24, 128), F32),
        ((4, 24, 128), F32),
        ((4, 8, 128), F32),
        ((2, 8, 128), F32),
        ((5, 8, 128), F32),
        ((12, 8, 128), F32),
        ((256, 128), F32),
        ((256, 128), F32),
        ((256, 128), F32),
        ((256, 128), F32),
        ((2, 256, 512), F32),
    ]
    out_t, loss = pl.pallas_call(
        kernel,
        out_shape=(
            jax.ShapeDtypeStruct((256, 512), BF),
            jax.ShapeDtypeStruct((8, 128), F32),
        ),
        in_specs=[hbm, vmem, hbm, hbm, vmem, hbm, hbm, vmem],
        out_specs=(vmem, vmem),
        scratch_shapes=[pltpu.VMEM(shape, kind) for shape, kind in scratch]
        + [
            pltpu.SemaphoreType.DMA((224,)),
            pltpu.SemaphoreType.DMA((224,)),
            pltpu.SemaphoreType.DMA((32,)),
            pltpu.SemaphoreType.DMA((6,)),
        ],
        compiler_params=pltpu.CompilerParams(
            collective_id=0, has_side_effects=True, vmem_limit_bytes=62 * 2**20
        ),
        cost_estimate=pl.CostEstimate(flops=26 * 10**9, bytes_accessed=16 * 2**20, transcendentals=0),
    )(
        teacher_hidden.reshape(8, 256, 1024),
        teacher_gain.reshape(1, 1024),
        target_proj.reshape(8, 128, D),
        student_in,
        student_gain.reshape(1, D),
        proj_weight,
        meta,
        wvec,
    )
    return loss[0, 64:72], out_t.T.astype(F32)


def solution(mesh):
    in_specs = (
        P("seq", "tp"),
        P("tp"),
        P("tp", None),
        P(("seq", "tp"), None),
        P(),
        P("seq", "tp"),
        P(("seq", "tp")),
        P(("seq", "tp")),
        P(),
    )
    out_specs = (P(), P("seq", "tp"))
    return jax.shard_map(shards, mesh=mesh, in_specs=in_specs, out_specs=out_specs, check_vma=False)
```

```python
import jax
import jax.numpy as jnp
from jax import lax
from jax.experimental import pallas as pl
from jax.experimental.pallas import tpu as pltpu
from jax.sharding import PartitionSpec as P

EPS = 1e-05
DT = 16384
D = 4096
NC = 4
SEMS = 160
SLOTS = 3
BF = jnp.bfloat16
F32 = jnp.float32
MESH = pl.DeviceIdType.MESH


def device(xh, z, y, xl, c):
    return {"seq": xh * 4 + z, "tp": (y * 2 + xl) * 2 + c}


def kernel(
    teacher,
    tgain,
    proj,
    student,
    sgain,
    weight,
    docs,
    streams,
    wstream,
    out_grad,
    out_loss,
    a_buf,
    b_buf,
    p_buf,
    r1_buf,
    r2_buf,
    sx_buf,
    rx_buf,
    nd_buf,
    w_buf,
    hs_buf,
    hr_buf,
    st_buf,
    gs_buf,
    gr_buf,
    gt_buf,
    dr1_buf,
    dr2_buf,
    ds_buf,
    dy_buf,
    fs_buf,
    fr_buf,
    m_buf,
    sq_buf,
    stat_buf,
    statr_buf,
    staty_buf,
    statz_buf,
    stato_buf,
    loss_buf,
    lossr_buf,
    rs_buf,
    sc_buf,
    ln_buf,
    te_buf,
    own_buf,
    sem,
    cross_sem,
):
    s = lax.axis_index("seq")
    t = lax.axis_index("tp")
    xh, z = s // 4, s % 4
    y, xl, c = t // 4, (t // 2) % 2, t % 2
    x = xh * 2 + xl
    o = 1 - c

    def at_y(k):
        return device(xh, z, (y + k) % 4, xl, c)

    def at_z(k):
        return device(xh, (z + k) % 4, y, xl, c)

    def at_x(k):
        n = (x + k) % 4
        return device(n // 2, z, y, n % 2, c)

    sibling = device(xh, z, y, xl, o)
    x_pair = device(xh, z, y, 1 - xl, c)
    x_outer = device(1 - xh, z, y, 1 - xl, c)

    used = [0]
    open_sends = []

    def new_sem():
        used[0] += 1
        return sem.at[used[0] - 1]

    class Group:
        def __init__(self, cover):
            self.cover, self.out, self.got = cover, new_sem(), new_sem()
            open_sends.append(self)

        def send(self, src, dst, to):
            pltpu.make_async_remote_copy(
                src_ref=src,
                dst_ref=dst,
                send_sem=self.out,
                recv_sem=self.got,
                device_id=to,
                device_id_type=MESH,
            ).start()
            return self

        def wait_recv(self):
            pltpu.make_async_copy(self.cover, self.cover, self.got).wait()

        def wait_send(self):
            pltpu.make_async_copy(self.cover, self.cover, self.out).wait()
            open_sends[:] = [other for other in open_sends if other is not self]

    def remote(src, dst, to):
        return Group(src).send(src, dst, to)

    class Load:
        def __init__(self, cover, pairs):
            self.cover, self.sem = cover, new_sem()
            for src, dst in pairs:
                pltpu.make_async_copy(src, dst, self.sem).start()

        def wait(self):
            pltpu.make_async_copy(self.cover, self.cover, self.sem).wait()

    def crossed(src, dst, to, itself, base):
        out = new_sem()
        cp = pltpu.make_async_remote_copy(
            src_ref=src,
            dst_ref=dst,
            send_sem=out,
            recv_sem=cross_sem.at[base + xl],
            device_id=to,
            device_id_type=MESH,
        )
        own = pltpu.make_async_copy(src, dst, cross_sem.at[base + xl])

        @pl.when(itself)
        def _():
            own.start()

        @pl.when(jnp.logical_not(itself))
        def _():
            cp.start()

        return cp, itself

    def crossed_sent(pair):
        cp, itself = pair

        @pl.when(jnp.logical_not(itself))
        def _():
            cp.wait_send()

    takers = [(k, r, device(xh, y, k, r, c)) for k in range(4) for r in range(2)]
    givers = [(k, r, device(xh, k, z, r, c)) for k in range(4) for r in range(2)]
    barrier = pltpu.get_barrier_semaphore()
    peers = [sibling, at_x(1), at_x(3)] + [at_y(k) for k in (1, 2, 3)] + [at_z(k) for k in (1, 2, 3)]
    for peer in peers:
        pl.semaphore_signal(barrier, inc=1, device_id=peer, device_id_type=MESH)

    for k, r, peer in givers:

        @pl.when(jnp.logical_not(jnp.logical_and(y == z, jnp.logical_and(k == z, r == xl))))
        def _(peer=peer):
            pl.semaphore_signal(barrier, inc=1, device_id=peer, device_id_type=MESH)

    st_load = Load(st_buf.at[c], [(student, st_buf.at[c])])
    order = [2, 3, 0, 1]

    def pair_of(core, k):
        return a_buf.at[core, pl.ds(((y + k) % 4) * 2, 2)]

    a_load = [
        Load(pair_of(c, k), [(teacher.at[pl.ds(((y + k) % 4) * 2, 2)], pair_of(c, k))]) for k in order
    ]

    def proj_cols(j, yp, core):
        lane = yp * 1024 + (j // 2) * 512 + (j % 2) * 128 + core * 256
        return proj.at[:, :, pl.ds(pl.multiple_of(lane, 128), 128)]

    b_load = [
        Load(
            b_buf.at[c, j],
            [(proj_cols(j, yp, c), b_buf.at[c, j, :, :, pl.ds(yp * 128, 128)]) for yp in range(4)],
        )
        for j in range(NC)
    ]

    sgain_f = sgain[...].astype(F32)
    sgain_f = jnp.concatenate([sgain_f[i : i + 1] for i in range(D // 128)], axis=1)
    st_load.wait()

    def norm_rows(i, _):
        rows = pl.ds(pl.multiple_of(i * 16, 16), 16)
        v = st_buf[c, rows, :].astype(F32)
        scale = lax.rsqrt(jnp.sum(v * v, axis=1, keepdims=True) / D + EPS)
        n = (v * scale * sgain_f).astype(BF)
        for p in range(4):
            for zp in range(4):
                src = (p // 2) * 2048 + zp * 512 + (p % 2) * 256
                nd_buf[z, c, rows, pl.ds(p * 1024 + zp * 256, 256)] = n[:, src : src + 256]
        return 0

    lax.fori_loop(0, 8, norm_rows, 0)

    @pl.when(y != z)
    def _():
        pl.semaphore_wait(barrier, len(peers) + 8)

    @pl.when(y == z)
    def _():
        pl.semaphore_wait(barrier, len(peers) + 7)

    w_swap = [
        crossed(
            weight.at[pl.ds(r * 256, 256)],
            w_buf.at[xh * 2 + r, z, :, pl.ds(pl.multiple_of(xl * 256, 128), 256)],
            peer,
            jnp.logical_and(y == z, jnp.logical_and(k == y, r == xl)),
            0,
        )
        for k, r, peer in takers
    ]

    def send_b(j):
        g = Group(b_buf.at[c, j])
        for yp in range(4):
            g.send(proj_cols(j, yp, o), b_buf.at[c, j, :, :, pl.ds(yp * 128, 128)], sibling)
        return g

    b_recv = [send_b(0)]

    def half(h):
        return pl.ds(h * 64, 64)

    nd_right, nd_left = [None, None], [None, None]
    for first in range(2):
        own = nd_buf.at[z, c, half(first)]
        nd_right[first] = remote(own, own, at_z(1))
        own = nd_buf.at[z, c, half(1 - first)]
        nd_left[1 - first] = remote(own, own, at_z(3))

    tgain_f = tgain[...].astype(F32)
    tgain_f = jnp.concatenate([tgain_f[i : i + 1] for i in range(8)], axis=1)
    ones = jnp.ones((8, 1024), BF)
    a_recv = []
    for load, k in zip(a_load, order):
        load.wait()

        def prep(r, _, k=k):
            b = ((y + k) % 4) * 2 + r // 2
            rows = pl.ds(pl.multiple_of((r % 2) * 128, 128), 128)
            v = a_buf[c, b, rows, :].astype(F32)
            squares = (v * v).astype(BF)
            sq_buf[((y + k) % 4) * 4 + r] = lax.dot_general(
                ones, squares, (((1,), (1,)), ((), ())), preferred_element_type=F32
            )
            a_buf[c, b, rows, :] = (v * tgain_f).astype(BF)
            return 0

        lax.fori_loop(0, 4, prep, 0)
        a_recv.append(remote(pair_of(c, k), pair_of(c, k), sibling))

    eye = lax.broadcasted_iota(jnp.int32, (128, 128), 0) == lax.broadcasted_iota(
        jnp.int32, (128, 128), 1
    )

    def column(row):
        return jnp.sum(jnp.where(eye, jnp.broadcast_to(row, (128, 128)), 0.0), axis=1, keepdims=True)

    lane = lax.broadcasted_iota(jnp.int32, (128, 128), 1).astype(F32)
    doc_col = column(docs[...].astype(F32)) + 64.0
    stream_col = column(streams[...].astype(F32))
    m_buf[c] = jnp.where(
        lane < 64.0, jnp.where(lane == stream_col, 1.0, 0.0), jnp.where(lane == doc_col, 1.0, 0.0)
    )
    m_recv = remote(m_buf.at[c], m_buf.at[c], sibling)

    def cols(h):
        return pl.ds(h * 256, 256)

    for j in range(1, NC):
        b_recv.append(send_b(j))
    st_recv = remote(st_buf.at[c], st_buf.at[c], sibling)
    nd_side = Group(nd_buf.at[:, c])

    def pass_on(k):
        whole = nd_buf.at[(z + k) % 4, c]
        nd_side.send(whole, whole, sibling)

    pass_on(0)

    for i in range(16):
        stat_buf[0, i : i + 1, :] = sq_buf[i, 0:1, :]
    own_counts = jnp.sum(m_buf[c], axis=0, keepdims=True)
    stat_buf[0, 16:24, :] = jnp.broadcast_to(own_counts, (8, 128))
    stat_c = remote(stat_buf.at[0], statr_buf.at[0], sibling)

    def part(k, h):
        return ((y + k) % 4) * 2 + h

    r1 = [None] * NC
    r2 = [None] * NC

    def stage_a(j):
        slot = j % SLOTS
        if j >= SLOTS:
            r1[j - SLOTS].wait_send()
            r2[j - SLOTS].wait_send()
        b_load[j].wait()
        b_recv[j].wait_recv()
        r1[j] = Group(r1_buf.at[j])
        r2[j] = Group(r2_buf.at[j])

        def body(i, _):
            if j == 0:
                for n in range(4):

                    @pl.when(i == 2 * n)
                    def _(n=n):
                        a_recv[n].wait_recv()

            b = (y * 2 + 4 + i) % 8
            acc = jnp.dot(a_buf[0, b], b_buf[0, j].reshape(1024, 512), preferred_element_type=F32)
            acc = acc + jnp.dot(
                a_buf[1, b], b_buf[1, j].reshape(1024, 512), preferred_element_type=F32
            )
            p_buf[slot, b] = acc.astype(BF)

            @pl.when(i == 0)
            def _():
                r1[j].send(p_buf.at[slot, part(2, 0)], r1_buf.at[j, 0], at_y(1))

            @pl.when(i == 1)
            def _():
                r1[j].send(p_buf.at[slot, part(2, 1)], r1_buf.at[j, 1], at_y(3))

            @pl.when(i == 2)
            def _():
                r2[j].send(p_buf.at[slot, part(3, 0)], r2_buf.at[j, 1, 0], at_y(3))

            @pl.when(i == 7)
            def _():
                r2[j].send(p_buf.at[slot, part(1, 1)], r2_buf.at[j, 0, 1], at_y(1))

            return 0

        lax.fori_loop(0, 8, body, 0)

    def stage_b(j):
        slot = j % SLOTS
        r1[j].wait_recv()
        for i, (k, h) in enumerate(((1, 0), (3, 1))):
            b = part(k, h)
            p_buf[slot, b] = (p_buf[slot, b].astype(F32) + r1_buf[j, i].astype(F32)).astype(BF)
            r2[j].send(p_buf.at[slot, b], r2_buf.at[j, i, h], at_y(k))

    def summed(j, h, lanes):
        slot = j % SLOTS
        return (
            p_buf[slot, part(0, h), :, lanes].astype(F32)
            + r2_buf[j, 0, h, :, lanes].astype(F32)
            + r2_buf[j, 1, h, :, lanes].astype(F32)
        )

    rx = [None] * NC

    def stage_c(j):
        r2[j].wait_recv()
        for i in range(4):
            lanes = pl.ds(i * 128, 128)
            sx_buf[j, :, lanes] = summed(j, 1 - xl, lanes).astype(BF)
        rx[j] = remote(sx_buf.at[j], rx_buf.at[j], x_pair)
        for i in range(4):
            lanes = pl.ds(i * 128, 128)
            own_buf[j % 2, :, lanes] = summed(j, xl, lanes)

    gr = [None] * NC

    def stage_d(j):
        rx[j].wait_recv()
        gr[j] = Group(gr_buf.at[j, pl.ds(0, 3)])
        for yp in range(4):
            lanes = pl.ds(yp * 128, 128)
            target = own_buf[j % 2, :, lanes] + rx_buf[j, :, lanes].astype(F32)
            lane0 = yp * 1024 + (j // 2) * 512 + (j % 2) * 128 + c * 256
            st = st_buf[:, :, pl.ds(pl.multiple_of(lane0, 128), 128)].reshape(256, 128)
            hidden = hr_buf[j // 2, yp, :, pl.ds((j % 2) * 128, 128)]
            error = st.astype(F32) + hidden.astype(F32) - target * rs_buf[...]
            if j == 0 and yp == 0:
                te_buf[...] = error * error
            else:
                te_buf[...] += error * error
            gs_buf[j, yp] = (error * sc_buf[...]).astype(BF)
        for k in (2, 1, 3):
            gr[j].send(gs_buf.at[j, (z + k) % 4], gr_buf.at[j, z], at_z(k))
        gr_buf[j, z] = gs_buf[j, z]

    d1 = [None] * NC
    d2 = [None] * NC

    def dpart(k, h):
        return ((x + k) % 4) * 2 + h

    def stage_e(j):
        gr[j].wait_recv()
        gt_buf[...] = gr_buf[j].reshape(1024, 128).T
        d1[j] = Group(dr1_buf.at[j])
        d2[j] = Group(dr2_buf.at[j])

        def body(i, _):
            b = (x * 2 + 4 + i) % 8
            lanes = pl.ds(pl.multiple_of(b * 512, 512), 512)
            nd = nd_buf[:, :, :, lanes].reshape(1024, 512)
            b_buf[0, j, b] = jnp.dot(gt_buf[...], nd, preferred_element_type=F32).astype(BF)

            @pl.when(i == 0)
            def _():
                d1[j].send(b_buf.at[0, j, dpart(2, 0)], dr1_buf.at[j, 0], at_x(1))

            @pl.when(i == 1)
            def _():
                d1[j].send(b_buf.at[0, j, dpart(2, 1)], dr1_buf.at[j, 1], at_x(3))

            @pl.when(i == 2)
            def _():
                d2[j].send(b_buf.at[0, j, dpart(3, 0)], dr2_buf.at[j, 1, 0], at_x(3))

            @pl.when(i == 7)
            def _():
                d2[j].send(b_buf.at[0, j, dpart(1, 1)], dr2_buf.at[j, 0, 1], at_x(1))

            return 0

        lax.fori_loop(0, 8, body, 0)

    def stage_f(j):
        d1[j].wait_recv()
        for i, (k, h) in enumerate(((1, 0), (3, 1))):
            b = dpart(k, h)
            b_buf[0, j, b] = (b_buf[0, j, b].astype(F32) + dr1_buf[j, i].astype(F32)).astype(BF)
            d2[j].send(b_buf.at[0, j, b], dr2_buf.at[j, i, h], at_x(k))

    dy = [None] * NC

    def stage_g(j):
        d2[j].wait_recv()
        for zp in range(4):
            h, lanes = zp // 2, pl.ds((zp % 2) * 256, 256)
            ds_buf[j, zp] = (
                b_buf[0, j, dpart(0, h), :, lanes].astype(F32)
                + dr2_buf[j, 0, h, :, lanes].astype(F32)
                + dr2_buf[j, 1, h, :, lanes].astype(F32)
            ).astype(BF)
        dy[j] = Group(dy_buf.at[j, pl.ds(0, 3)])
        for k in (2, 1, 3):
            dy[j].send(ds_buf.at[j, (y + k) % 4], dy_buf.at[j, y], at_y(k))

    final = [None] * NC

    def stage_h(j):
        dy[j].wait_recv()
        total = ds_buf[j, y].astype(F32)
        for k in (1, 2, 3):
            total = total + dy_buf[j, (y + k) % 4].astype(F32)
        fs_buf[j] = total.astype(BF)
        final[j] = crossed(
            fs_buf.at[j],
            fr_buf.at[j % 2, xl],
            device(xh, y, z, j // 2, c),
            jnp.logical_and(y == z, xl == j // 2),
            2 + 2 * (j % 2),
        )

    w_x = [None, None]

    def gather_x1(h):
        own = w_buf.at[x, :, :, cols(h)]
        pltpu.make_async_copy(own, own, cross_sem.at[h]).wait()
        w_x[h] = Group(w_buf.at[pl.ds(0, 2), :, :, cols(h)])
        for k in (1, 3):
            w_x[h].send(own, own, at_x(k))

    w_f = [None, None]

    def gather_x2(h):
        w_x[h].wait_recv()
        w_f[h] = Group(w_buf.at[0, :, :, cols(h)])
        left = w_buf.at[(x + 3) % 4, pl.ds(0, 2), :, cols(h)]
        w_f[h].send(left, left, at_x(1))
        right = w_buf.at[(x + 1) % 4, pl.ds(2, 2), :, cols(h)]
        w_f[h].send(right, right, at_x(3))

    hr = [None, None]

    def hidden_half(h):
        w_f[h].wait_recv()
        hr[h] = Group(hr_buf.at[h, pl.ds(0, 3)])

        def body(i, _):
            zd = (z + 1 + i) % 4
            hs_buf[h, zd] = jnp.dot(
                nd_buf[zd].reshape(256, D),
                w_buf[:, :, :, cols(h)].reshape(D, 256),
                preferred_element_type=F32,
            ).astype(BF)

            @pl.when(i < 3)
            def _():
                hr[h].send(hs_buf.at[h, zd], hr_buf.at[h, z], device(xh, zd, y, xl, c))

            return 0

        lax.fori_loop(0, 4, body, 0)
        hr_buf[h, z] = hs_buf[h, z]

    def loss_of(core):
        rows = pl.ds(core * 128, 128)
        te = jnp.sum(te_buf[rows], axis=1, keepdims=True) / D
        return jnp.sum(m_buf[core] * (te / ln_buf[rows]), axis=0, keepdims=True)

    stage_a(0)
    gather_x1(0)
    gather_x1(1)
    nd_right[0].wait_recv()
    nd_far = Group(nd_buf.at[z, c])
    from_left = nd_buf.at[(z + 3) % 4, c, half(0)]
    nd_far.send(from_left, from_left, at_z(1))
    nd_left[1].wait_recv()
    from_right = nd_buf.at[(z + 1) % 4, c, half(1)]
    nd_far.send(from_right, from_right, at_z(3))
    stat_c.wait_recv()
    stat_buf[1] = stat_buf[0] + statr_buf[0]
    stat_x = remote(stat_buf.at[1], statr_buf.at[1], x_pair)
    stage_a(1)
    stat_x.wait_recv()
    stat_buf[2] = stat_buf[1] + statr_buf[1]
    stat_y = Group(staty_buf.at[pl.ds(0, 3)])
    for k in (1, 2, 3):
        stat_y.send(stat_buf.at[2], staty_buf.at[y], at_y(k))
    staty_buf[y] = stat_buf[2]
    stage_b(0)
    stage_a(2)
    gather_x2(0)
    stat_y.wait_recv()
    stat = staty_buf[0] + staty_buf[1] + staty_buf[2] + staty_buf[3]
    stat_buf[3] = stat
    statz_buf[z] = stat[16:24]
    stat_z = Group(statz_buf.at[pl.ds(0, 3)])
    for k in (1, 2, 3):
        stat_z.send(stat_buf.at[3, pl.ds(16, 8)], statz_buf.at[z], at_z(k))
    nd_right[1].wait_recv()
    nd_left[0].wait_recv()
    pass_on(3)
    pass_on(1)
    stage_b(1)
    stage_c(0)
    stage_a(3)
    stat_z.wait_recv()
    stato_buf[0] = statz_buf[0] + statz_buf[1] + statz_buf[2] + statz_buf[3]
    stat_o = remote(stato_buf.at[0], stato_buf.at[1], x_outer)
    gather_x2(1)
    nd_far.wait_recv()
    pass_on(2)
    stage_b(2)

    stat_o.wait_recv()
    m_recv.wait_recv()
    lane1 = lax.broadcasted_iota(jnp.int32, (8, 128), 1)
    doc_counts = jnp.where(lane1 >= 64, stato_buf[0] + stato_buf[1], 0.0)[0:1]
    stream_w = jnp.zeros((8, 128), F32)
    for i in range(8):
        stream_w = jnp.where(lane1 == i, wstream[i], stream_w)
    stream_w = stream_w[0:1]
    rows_i = lax.broadcasted_iota(jnp.int32, (24, 128), 0)
    for core in range(2):
        rows = pl.ds(core * 128, 128)
        row = jnp.sum(
            jnp.where(rows_i == (y * 2 + xl) * 2 + core, stat_buf[3], 0.0), axis=0, keepdims=True
        )
        rs_buf[rows] = jnp.broadcast_to(lax.rsqrt(column(row) / DT + EPS), (128, 128))
        m = m_buf[core]
        length = jnp.sum(m * doc_counts, axis=1, keepdims=True)
        sw = jnp.sum(m * stream_w, axis=1, keepdims=True)
        sc_buf[rows] = jnp.broadcast_to(2.0 * sw / length, (128, 128))
        ln_buf[rows] = jnp.broadcast_to(length, (128, 128))
    st_recv.wait_recv()

    nd_side.wait_recv()
    hidden_half(0)
    stage_c(1)
    stage_b(3)
    hr[0].wait_recv()
    stage_d(0)
    stage_d(1)
    hidden_half(1)
    stage_e(0)
    stage_e(1)
    stage_f(0)
    stage_c(2)
    hr[1].wait_recv()
    stage_d(2)
    stage_f(1)
    stage_e(2)
    stage_c(3)
    stage_f(2)
    stage_g(0)
    stage_g(1)
    stage_d(3)
    loss_buf[0] = jnp.broadcast_to(loss_of(0) + loss_of(1), (8, 128))
    loss_c = remote(loss_buf.at[0], lossr_buf.at[0], sibling)
    stage_h(0)
    stage_e(3)
    stage_g(2)
    stage_h(1)
    loss_c.wait_recv()
    loss_buf[1] = loss_buf[0] + lossr_buf[0]
    loss_x = remote(loss_buf.at[1], lossr_buf.at[1], x_pair)
    stage_f(3)
    stage_h(2)
    loss_x.wait_recv()
    loss_buf[2] = loss_buf[1] + lossr_buf[1]
    lossr_buf[4 + y] = loss_buf[2]
    loss_y = Group(lossr_buf.at[pl.ds(4, 3)])
    for k in (1, 2, 3):
        loss_y.send(loss_buf.at[2], lossr_buf.at[4 + y], at_y(k))
    stage_g(3)
    loss_y.wait_recv()
    loss_buf[3] = lossr_buf[4] + lossr_buf[5] + lossr_buf[6] + lossr_buf[7]
    lossr_buf[8 + z] = loss_buf[3]
    loss_z = Group(lossr_buf.at[pl.ds(8, 3)])
    for k in (1, 2, 3):
        loss_z.send(loss_buf.at[3], lossr_buf.at[8 + z], at_z(k))
    stage_h(3)
    loss_z.wait_recv()
    loss_buf[4] = lossr_buf[8] + lossr_buf[9] + lossr_buf[10] + lossr_buf[11]
    loss_o = remote(loss_buf.at[4], lossr_buf.at[2], x_outer)
    for group in list(open_sends):
        group.wait_send()
    for pair in w_swap + final:
        crossed_sent(pair)
    loss_o.wait_recv()
    out_loss[...] = (loss_buf[4] + lossr_buf[2])[0:1, 0:8]

    for jj in range(2):
        for r in range(2):
            got = fr_buf.at[jj, r]
            pltpu.make_async_copy(got, got, cross_sem.at[2 + 2 * jj + r]).wait()
            out_grad[pl.ds(r * 256, 256), pl.ds(jj * 128, 128)] = fr_buf[jj, r].astype(F32).T
    assert used[0] <= SEMS, used[0]


def shards(
    teacher_hidden,
    teacher_gain,
    target_proj,
    student_in,
    student_gain,
    proj_weight,
    doc_ids,
    stream_ids,
    stream_weight,
):
    hbm = pl.BlockSpec(memory_space=pl.ANY)
    vmem = pl.BlockSpec(memory_space=pltpu.VMEM)
    scratch = [
        ((2, 8, 256, 1024), BF),
        ((2, NC, 8, 128, 512), BF),
        ((SLOTS, 8, 256, 512), BF),
        ((NC, 2, 256, 512), BF),
        ((NC, 2, 2, 256, 512), BF),
        ((NC, 256, 512), BF),
        ((NC, 256, 512), BF),
        ((4, 2, 128, D), BF),
        ((4, 4, 256, 512), BF),
        ((2, 4, 256, 256), BF),
        ((2, 4, 256, 256), BF),
        ((2, 128, D), BF),
        ((NC, 4, 256, 128), BF),
        ((NC, 4, 256, 128), BF),
        ((128, 1024), BF),
        ((NC, 2, 128, 512), BF),
        ((NC, 2, 2, 128, 512), BF),
        ((NC, 4, 128, 256), BF),
        ((NC, 4, 128, 256), BF),
        ((NC, 128, 256), BF),
        ((2, 2, 128, 256), BF),
        ((2, 128, 128), F32),
        ((16, 8, 128), F32),
        ((4, 24, 128), F32),
        ((2, 24, 128), F32),
        ((4, 24, 128), F32),
        ((4, 8, 128), F32),
        ((2, 8, 128), F32),
        ((5, 8, 128), F32),
        ((12, 8, 128), F32),
        ((256, 128), F32),
        ((256, 128), F32),
        ((256, 128), F32),
        ((256, 128), F32),
        ((2, 256, 512), F32),
    ]
    w_grad, loss = pl.pallas_call(
        kernel,
        out_shape=(
            jax.ShapeDtypeStruct((512, 256), F32),
            jax.ShapeDtypeStruct((1, 8), F32),
        ),
        in_specs=[hbm, vmem, hbm, hbm, vmem, hbm, vmem, vmem, pl.BlockSpec(memory_space=pltpu.SMEM)],
        out_specs=(vmem, vmem),
        scratch_shapes=[pltpu.VMEM(shape, kind) for shape, kind in scratch]
        + [pltpu.SemaphoreType.DMA((SEMS,)), pltpu.SemaphoreType.DMA((6,))],
        compiler_params=pltpu.CompilerParams(
            collective_id=0, has_side_effects=True, vmem_limit_bytes=62 * 2**20
        ),
        cost_estimate=pl.CostEstimate(flops=26 * 10**9, bytes_accessed=16 * 2**20, transcendentals=0),
    )(
        teacher_hidden.reshape(8, 256, 1024),
        teacher_gain.reshape(8, 128),
        target_proj.reshape(8, 128, D),
        student_in,
        student_gain.reshape(D // 128, 128),
        proj_weight,
        doc_ids.reshape(1, 128),
        stream_ids.reshape(1, 128),
        stream_weight,
    )
    return loss.reshape(8), w_grad


def solution(mesh):
    in_specs = (
        P("seq", "tp"),
        P("tp"),
        P("tp", None),
        P(("seq", "tp"), None),
        P(),
        P("seq", "tp"),
        P(("seq", "tp")),
        P(("seq", "tp")),
        P(),
    )
    out_specs = (P(), P("seq", "tp"))
    return jax.shard_map(shards, mesh=mesh, in_specs=in_specs, out_specs=out_specs, check_vma=False)
```

```python
import jax
import jax.numpy as jnp
from jax import lax
from jax.experimental import pallas as pl
from jax.experimental.pallas import tpu as pltpu
from jax.sharding import PartitionSpec as P

EPS = 1e-05
DT = 16384
D = 4096
NC = 4
SEMS = 160
SLOTS = 3
BF = jnp.bfloat16
F32 = jnp.float32
MESH = pl.DeviceIdType.MESH
SCHEDULE = (
    "A0", "X0", "X1", "N1", "S1", "A1", "S2", "B0", "A2", "Y0", "S3", "N2",
    "B1", "C0", "A3", "S4", "Y1", "N3", "B2", "S5", "N4", "Q0", "C1", "B3",
    "R0", "D0", "Q1", "E0", "D1", "F0", "C2", "E1", "R1", "D2", "F1", "C3",
    "E2", "G0", "F2", "D3", "L1", "G1", "H0", "E3", "G2", "H1", "L2", "F3",
    "H2", "L3", "G3", "L4", "H3", "L5",
)


def device(xh, z, y, xl, c):
    return {"seq": xh * 4 + z, "tp": (y * 2 + xl) * 2 + c}


def kernel(
    teacher,
    tgain,
    proj,
    student,
    sgain,
    weight,
    docs,
    streams,
    wstream,
    out_grad,
    out_loss,
    a_buf,
    b_buf,
    p_buf,
    r1_buf,
    r2_buf,
    sx_buf,
    rx_buf,
    nd_buf,
    w_buf,
    hs_buf,
    hr_buf,
    st_buf,
    gs_buf,
    gr_buf,
    gt_buf,
    dr1_buf,
    dr2_buf,
    ds_buf,
    dy_buf,
    fs_buf,
    fr_buf,
    m_buf,
    sq_buf,
    stat_buf,
    statr_buf,
    staty_buf,
    statz_buf,
    stato_buf,
    loss_buf,
    lossr_buf,
    rs_buf,
    sc_buf,
    ln_buf,
    te_buf,
    own_buf,
    sem,
    cross_sem,
):
    s = lax.axis_index("seq")
    t = lax.axis_index("tp")
    xh, z = s // 4, s % 4
    y, xl, c = t // 4, (t // 2) % 2, t % 2
    x = xh * 2 + xl
    o = 1 - c

    def at_y(k):
        return device(xh, z, (y + k) % 4, xl, c)

    def at_z(k):
        return device(xh, (z + k) % 4, y, xl, c)

    def at_x(k):
        n = (x + k) % 4
        return device(n // 2, z, y, n % 2, c)

    sibling = device(xh, z, y, xl, o)
    x_pair = device(xh, z, y, 1 - xl, c)
    x_outer = device(1 - xh, z, y, 1 - xl, c)

    used = [0]
    open_sends = []

    def new_sem():
        used[0] += 1
        return sem.at[used[0] - 1]

    class Group:
        def __init__(self, cover):
            self.cover, self.out, self.got = cover, new_sem(), new_sem()
            open_sends.append(self)

        def send(self, src, dst, to):
            pltpu.make_async_remote_copy(
                src_ref=src,
                dst_ref=dst,
                send_sem=self.out,
                recv_sem=self.got,
                device_id=to,
                device_id_type=MESH,
            ).start()
            return self

        def wait_recv(self):
            pltpu.make_async_copy(self.cover, self.cover, self.got).wait()

        def wait_send(self):
            pltpu.make_async_copy(self.cover, self.cover, self.out).wait()
            open_sends[:] = [other for other in open_sends if other is not self]

    def remote(src, dst, to):
        return Group(src).send(src, dst, to)

    class Load:
        def __init__(self, cover, pairs):
            self.cover, self.sem = cover, new_sem()
            for src, dst in pairs:
                pltpu.make_async_copy(src, dst, self.sem).start()

        def wait(self):
            pltpu.make_async_copy(self.cover, self.cover, self.sem).wait()

    def crossed(src, dst, to, itself, base):
        out = new_sem()
        cp = pltpu.make_async_remote_copy(
            src_ref=src,
            dst_ref=dst,
            send_sem=out,
            recv_sem=cross_sem.at[base + xl],
            device_id=to,
            device_id_type=MESH,
        )
        own = pltpu.make_async_copy(src, dst, cross_sem.at[base + xl])

        @pl.when(itself)
        def _():
            own.start()

        @pl.when(jnp.logical_not(itself))
        def _():
            cp.start()

        return cp, itself

    def crossed_sent(pair):
        cp, itself = pair

        @pl.when(jnp.logical_not(itself))
        def _():
            cp.wait_send()

    takers = [(k, r, device(xh, y, k, r, c)) for k in range(4) for r in range(2)]
    givers = [(k, r, device(xh, k, z, r, c)) for k in range(4) for r in range(2)]
    barrier = pltpu.get_barrier_semaphore()
    peers = [sibling, at_x(1), at_x(3)] + [at_y(k) for k in (1, 2, 3)] + [at_z(k) for k in (1, 2, 3)]
    for peer in peers:
        pl.semaphore_signal(barrier, inc=1, device_id=peer, device_id_type=MESH)

    for k, r, peer in givers:

        @pl.when(jnp.logical_not(jnp.logical_and(y == z, jnp.logical_and(k == z, r == xl))))
        def _(peer=peer):
            pl.semaphore_signal(barrier, inc=1, device_id=peer, device_id_type=MESH)

    st_load = Load(st_buf.at[c], [(student, st_buf.at[c])])
    order = [2, 3, 0, 1]

    def pair_of(core, k):
        return a_buf.at[core, pl.ds(((y + k) % 4) * 2, 2)]

    a_load = [
        Load(pair_of(c, k), [(teacher.at[pl.ds(((y + k) % 4) * 2, 2)], pair_of(c, k))]) for k in order
    ]

    def proj_cols(j, yp, core):
        lane = yp * 1024 + (j // 2) * 512 + (j % 2) * 128 + core * 256
        return proj.at[:, :, pl.ds(pl.multiple_of(lane, 128), 128)]

    b_load = [
        Load(
            b_buf.at[c, j],
            [(proj_cols(j, yp, c), b_buf.at[c, j, :, :, pl.ds(yp * 128, 128)]) for yp in range(4)],
        )
        for j in range(NC)
    ]

    sgain_f = sgain[...].astype(F32)
    sgain_f = jnp.concatenate([sgain_f[i : i + 1] for i in range(D // 128)], axis=1)
    st_load.wait()

    def norm_rows(i, _):
        rows = pl.ds(pl.multiple_of(i * 16, 16), 16)
        v = st_buf[c, rows, :].astype(F32)
        scale = lax.rsqrt(jnp.sum(v * v, axis=1, keepdims=True) / D + EPS)
        n = (v * scale * sgain_f).astype(BF)
        for p in range(4):
            for zp in range(4):
                src = (p // 2) * 2048 + zp * 512 + (p % 2) * 256
                nd_buf[z, c, rows, pl.ds(p * 1024 + zp * 256, 256)] = n[:, src : src + 256]
        return 0

    lax.fori_loop(0, 8, norm_rows, 0)

    @pl.when(y != z)
    def _():
        pl.semaphore_wait(barrier, len(peers) + 8)

    @pl.when(y == z)
    def _():
        pl.semaphore_wait(barrier, len(peers) + 7)

    w_swap = [
        crossed(
            weight.at[pl.ds(r * 256, 256)],
            w_buf.at[xh * 2 + r, z, :, pl.ds(pl.multiple_of(xl * 256, 128), 256)],
            peer,
            jnp.logical_and(y == z, jnp.logical_and(k == y, r == xl)),
            0,
        )
        for k, r, peer in takers
    ]

    def send_b(j):
        g = Group(b_buf.at[c, j])
        for yp in range(4):
            g.send(proj_cols(j, yp, o), b_buf.at[c, j, :, :, pl.ds(yp * 128, 128)], sibling)
        return g

    b_recv = [send_b(0)]

    def half(h):
        return pl.ds(h * 64, 64)

    nd_right, nd_left = [None, None], [None, None]
    for first in range(2):
        own = nd_buf.at[z, c, half(first)]
        nd_right[first] = remote(own, own, at_z(1))
        own = nd_buf.at[z, c, half(1 - first)]
        nd_left[1 - first] = remote(own, own, at_z(3))

    tgain_f = tgain[...].astype(F32)
    tgain_f = jnp.concatenate([tgain_f[i : i + 1] for i in range(8)], axis=1)
    ones = jnp.ones((8, 1024), BF)
    a_recv = []
    for load, k in zip(a_load, order):
        load.wait()

        def prep(r, _, k=k):
            b = ((y + k) % 4) * 2 + r // 2
            rows = pl.ds(pl.multiple_of((r % 2) * 128, 128), 128)
            v = a_buf[c, b, rows, :].astype(F32)
            squares = (v * v).astype(BF)
            sq_buf[((y + k) % 4) * 4 + r] = lax.dot_general(
                ones, squares, (((1,), (1,)), ((), ())), preferred_element_type=F32
            )
            a_buf[c, b, rows, :] = (v * tgain_f).astype(BF)
            return 0

        lax.fori_loop(0, 4, prep, 0)
        a_recv.append(remote(pair_of(c, k), pair_of(c, k), sibling))

    eye = lax.broadcasted_iota(jnp.int32, (128, 128), 0) == lax.broadcasted_iota(
        jnp.int32, (128, 128), 1
    )

    def column(row):
        return jnp.sum(jnp.where(eye, jnp.broadcast_to(row, (128, 128)), 0.0), axis=1, keepdims=True)

    lane = lax.broadcasted_iota(jnp.int32, (128, 128), 1).astype(F32)
    doc_col = column(docs[...].astype(F32)) + 64.0
    stream_col = column(streams[...].astype(F32))
    m_buf[c] = jnp.where(
        lane < 64.0, jnp.where(lane == stream_col, 1.0, 0.0), jnp.where(lane == doc_col, 1.0, 0.0)
    )
    m_recv = remote(m_buf.at[c], m_buf.at[c], sibling)

    def cols(h):
        return pl.ds(h * 256, 256)

    for j in range(1, NC):
        b_recv.append(send_b(j))
    st_recv = remote(st_buf.at[c], st_buf.at[c], sibling)
    nd_side = Group(nd_buf.at[:, c])

    def pass_on(k):
        whole = nd_buf.at[(z + k) % 4, c]
        nd_side.send(whole, whole, sibling)

    pass_on(0)

    for i in range(16):
        stat_buf[0, i : i + 1, :] = sq_buf[i, 0:1, :]
    own_counts = jnp.sum(m_buf[c], axis=0, keepdims=True)
    stat_buf[0, 16:24, :] = jnp.broadcast_to(own_counts, (8, 128))
    stat_c = remote(stat_buf.at[0], statr_buf.at[0], sibling)

    def part(k, h):
        return ((y + k) % 4) * 2 + h

    r1 = [None] * NC
    r2 = [None] * NC

    def stage_a(j):
        slot = j % SLOTS
        if j >= SLOTS:
            r1[j - SLOTS].wait_send()
            r2[j - SLOTS].wait_send()
        b_load[j].wait()
        b_recv[j].wait_recv()
        r1[j] = Group(r1_buf.at[j])
        r2[j] = Group(r2_buf.at[j])

        def body(i, _):
            if j == 0:
                for n in range(4):

                    @pl.when(i == 2 * n)
                    def _(n=n):
                        a_recv[n].wait_recv()

            b = (y * 2 + 4 + i) % 8
            acc = jnp.dot(a_buf[0, b], b_buf[0, j].reshape(1024, 512), preferred_element_type=F32)
            acc = acc + jnp.dot(
                a_buf[1, b], b_buf[1, j].reshape(1024, 512), preferred_element_type=F32
            )
            p_buf[slot, b] = acc.astype(BF)

            @pl.when(i == 0)
            def _():
                r1[j].send(p_buf.at[slot, part(2, 0)], r1_buf.at[j, 0], at_y(1))

            @pl.when(i == 1)
            def _():
                r1[j].send(p_buf.at[slot, part(2, 1)], r1_buf.at[j, 1], at_y(3))

            @pl.when(i == 2)
            def _():
                r2[j].send(p_buf.at[slot, part(3, 0)], r2_buf.at[j, 1, 0], at_y(3))

            @pl.when(i == 7)
            def _():
                r2[j].send(p_buf.at[slot, part(1, 1)], r2_buf.at[j, 0, 1], at_y(1))

            return 0

        lax.fori_loop(0, 8, body, 0)

    def stage_b(j):
        slot = j % SLOTS
        r1[j].wait_recv()
        for i, (k, h) in enumerate(((1, 0), (3, 1))):
            b = part(k, h)
            p_buf[slot, b] = (p_buf[slot, b].astype(F32) + r1_buf[j, i].astype(F32)).astype(BF)
            r2[j].send(p_buf.at[slot, b], r2_buf.at[j, i, h], at_y(k))

    def summed(j, h, lanes):
        slot = j % SLOTS
        return (
            p_buf[slot, part(0, h), :, lanes].astype(F32)
            + r2_buf[j, 0, h, :, lanes].astype(F32)
            + r2_buf[j, 1, h, :, lanes].astype(F32)
        )

    rx = [None] * NC

    def stage_c(j):
        r2[j].wait_recv()
        for i in range(4):
            lanes = pl.ds(i * 128, 128)
            sx_buf[j, :, lanes] = summed(j, 1 - xl, lanes).astype(BF)
        rx[j] = remote(sx_buf.at[j], rx_buf.at[j], x_pair)
        for i in range(4):
            lanes = pl.ds(i * 128, 128)
            own_buf[j % 2, :, lanes] = summed(j, xl, lanes)

    gr = [None] * NC

    def stage_d(j):
        rx[j].wait_recv()
        gr[j] = Group(gr_buf.at[j, pl.ds(0, 3)])
        for yp in range(4):
            lanes = pl.ds(yp * 128, 128)
            target = own_buf[j % 2, :, lanes] + rx_buf[j, :, lanes].astype(F32)
            lane0 = yp * 1024 + (j // 2) * 512 + (j % 2) * 128 + c * 256
            st = st_buf[:, :, pl.ds(pl.multiple_of(lane0, 128), 128)].reshape(256, 128)
            hidden = hr_buf[j // 2, yp, :, pl.ds((j % 2) * 128, 128)]
            error = st.astype(F32) + hidden.astype(F32) - target * rs_buf[...]
            if j == 0 and yp == 0:
                te_buf[...] = error * error
            else:
                te_buf[...] += error * error
            gs_buf[j, yp] = (error * sc_buf[...]).astype(BF)
        for k in (2, 1, 3):
            gr[j].send(gs_buf.at[j, (z + k) % 4], gr_buf.at[j, z], at_z(k))
        gr_buf[j, z] = gs_buf[j, z]

    d1 = [None] * NC
    d2 = [None] * NC

    def dpart(k, h):
        return ((x + k) % 4) * 2 + h

    def stage_e(j):
        gr[j].wait_recv()
        gt_buf[...] = gr_buf[j].reshape(1024, 128).T
        d1[j] = Group(dr1_buf.at[j])
        d2[j] = Group(dr2_buf.at[j])

        def body(i, _):
            b = (x * 2 + 4 + i) % 8
            lanes = pl.ds(pl.multiple_of(b * 512, 512), 512)
            nd = nd_buf[:, :, :, lanes].reshape(1024, 512)
            b_buf[0, j, b] = jnp.dot(gt_buf[...], nd, preferred_element_type=F32).astype(BF)

            @pl.when(i == 0)
            def _():
                d1[j].send(b_buf.at[0, j, dpart(2, 0)], dr1_buf.at[j, 0], at_x(1))

            @pl.when(i == 1)
            def _():
                d1[j].send(b_buf.at[0, j, dpart(2, 1)], dr1_buf.at[j, 1], at_x(3))

            @pl.when(i == 2)
            def _():
                d2[j].send(b_buf.at[0, j, dpart(3, 0)], dr2_buf.at[j, 1, 0], at_x(3))

            @pl.when(i == 7)
            def _():
                d2[j].send(b_buf.at[0, j, dpart(1, 1)], dr2_buf.at[j, 0, 1], at_x(1))

            return 0

        lax.fori_loop(0, 8, body, 0)

    def stage_f(j):
        d1[j].wait_recv()
        for i, (k, h) in enumerate(((1, 0), (3, 1))):
            b = dpart(k, h)
            b_buf[0, j, b] = (b_buf[0, j, b].astype(F32) + dr1_buf[j, i].astype(F32)).astype(BF)
            d2[j].send(b_buf.at[0, j, b], dr2_buf.at[j, i, h], at_x(k))

    dy = [None] * NC

    def stage_g(j):
        d2[j].wait_recv()
        for zp in range(4):
            h, lanes = zp // 2, pl.ds((zp % 2) * 256, 256)
            ds_buf[j, zp] = (
                b_buf[0, j, dpart(0, h), :, lanes].astype(F32)
                + dr2_buf[j, 0, h, :, lanes].astype(F32)
                + dr2_buf[j, 1, h, :, lanes].astype(F32)
            ).astype(BF)
        dy[j] = Group(dy_buf.at[j, pl.ds(0, 3)])
        for k in (2, 1, 3):
            dy[j].send(ds_buf.at[j, (y + k) % 4], dy_buf.at[j, y], at_y(k))

    final = [None] * NC

    def stage_h(j):
        dy[j].wait_recv()
        total = ds_buf[j, y].astype(F32)
        for k in (1, 2, 3):
            total = total + dy_buf[j, (y + k) % 4].astype(F32)
        fs_buf[j] = total.astype(BF)
        final[j] = crossed(
            fs_buf.at[j],
            fr_buf.at[j % 2, xl],
            device(xh, y, z, j // 2, c),
            jnp.logical_and(y == z, xl == j // 2),
            2 + 2 * (j % 2),
        )

    w_x = [None, None]

    def gather_x1(h):
        own = w_buf.at[x, :, :, cols(h)]
        pltpu.make_async_copy(own, own, cross_sem.at[h]).wait()
        w_x[h] = Group(w_buf.at[pl.ds(0, 2), :, :, cols(h)])
        for k in (1, 3):
            w_x[h].send(own, own, at_x(k))

    w_f = [None, None]

    def gather_x2(h):
        w_x[h].wait_recv()
        w_f[h] = Group(w_buf.at[0, :, :, cols(h)])
        left = w_buf.at[(x + 3) % 4, pl.ds(0, 2), :, cols(h)]
        w_f[h].send(left, left, at_x(1))
        right = w_buf.at[(x + 1) % 4, pl.ds(2, 2), :, cols(h)]
        w_f[h].send(right, right, at_x(3))

    hr = [None, None]

    def hidden_half(h):
        w_f[h].wait_recv()
        hr[h] = Group(hr_buf.at[h, pl.ds(0, 3)])

        def body(i, _):
            zd = (z + 1 + i) % 4
            hs_buf[h, zd] = jnp.dot(
                nd_buf[zd].reshape(256, D),
                w_buf[:, :, :, cols(h)].reshape(D, 256),
                preferred_element_type=F32,
            ).astype(BF)

            @pl.when(i < 3)
            def _():
                hr[h].send(hs_buf.at[h, zd], hr_buf.at[h, z], device(xh, zd, y, xl, c))

            return 0

        lax.fori_loop(0, 4, body, 0)
        hr_buf[h, z] = hs_buf[h, z]

    def loss_of(core):
        rows = pl.ds(core * 128, 128)
        te = jnp.sum(te_buf[rows], axis=1, keepdims=True) / D
        return jnp.sum(m_buf[core] * (te / ln_buf[rows]), axis=0, keepdims=True)

    far = Group(nd_buf.at[z, c])

    def rows_second():
        nd_right[0].wait_recv()
        from_left = nd_buf.at[(z + 3) % 4, c, half(0)]
        far.send(from_left, from_left, at_z(1))
        nd_left[1].wait_recv()
        from_right = nd_buf.at[(z + 1) % 4, c, half(1)]
        far.send(from_right, from_right, at_z(3))

    def rows_near():
        nd_right[1].wait_recv()
        nd_left[0].wait_recv()
        pass_on(3)
        pass_on(1)

    def rows_far():
        far.wait_recv()
        pass_on(2)

    kept = {}

    def stat_1():
        stat_c.wait_recv()
        stat_buf[1] = stat_buf[0] + statr_buf[0]
        kept["x"] = remote(stat_buf.at[1], statr_buf.at[1], x_pair)

    def stat_2():
        kept["x"].wait_recv()
        stat_buf[2] = stat_buf[1] + statr_buf[1]
        kept["y"] = Group(staty_buf.at[pl.ds(0, 3)])
        for k in (1, 2, 3):
            kept["y"].send(stat_buf.at[2], staty_buf.at[y], at_y(k))
        staty_buf[y] = stat_buf[2]

    def stat_3():
        kept["y"].wait_recv()
        stat = staty_buf[0] + staty_buf[1] + staty_buf[2] + staty_buf[3]
        stat_buf[3] = stat
        statz_buf[z] = stat[16:24]
        kept["z"] = Group(statz_buf.at[pl.ds(0, 3)])
        for k in (1, 2, 3):
            kept["z"].send(stat_buf.at[3, pl.ds(16, 8)], statz_buf.at[z], at_z(k))

    def stat_4():
        kept["z"].wait_recv()
        stato_buf[0] = statz_buf[0] + statz_buf[1] + statz_buf[2] + statz_buf[3]
        kept["o"] = remote(stato_buf.at[0], stato_buf.at[1], x_outer)

    def scales():
        kept["o"].wait_recv()
        m_recv.wait_recv()
        lane1 = lax.broadcasted_iota(jnp.int32, (8, 128), 1)
        doc_counts = jnp.where(lane1 >= 64, stato_buf[0] + stato_buf[1], 0.0)[0:1]
        stream_w = jnp.zeros((8, 128), F32)
        for i in range(8):
            stream_w = jnp.where(lane1 == i, wstream[i], stream_w)
        stream_w = stream_w[0:1]
        rows_i = lax.broadcasted_iota(jnp.int32, (24, 128), 0)
        for core in range(2):
            rows = pl.ds(core * 128, 128)
            row = jnp.sum(
                jnp.where(rows_i == (y * 2 + xl) * 2 + core, stat_buf[3], 0.0),
                axis=0,
                keepdims=True,
            )
            rs_buf[rows] = jnp.broadcast_to(lax.rsqrt(column(row) / DT + EPS), (128, 128))
            m = m_buf[core]
            length = jnp.sum(m * doc_counts, axis=1, keepdims=True)
            sw = jnp.sum(m * stream_w, axis=1, keepdims=True)
            sc_buf[rows] = jnp.broadcast_to(2.0 * sw / length, (128, 128))
            ln_buf[rows] = jnp.broadcast_to(length, (128, 128))
        st_recv.wait_recv()

    def loss_1():
        loss_buf[0] = jnp.broadcast_to(loss_of(0) + loss_of(1), (8, 128))
        kept["lc"] = remote(loss_buf.at[0], lossr_buf.at[0], sibling)

    def loss_2():
        kept["lc"].wait_recv()
        loss_buf[1] = loss_buf[0] + lossr_buf[0]
        kept["lx"] = remote(loss_buf.at[1], lossr_buf.at[1], x_pair)

    def loss_3():
        kept["lx"].wait_recv()
        loss_buf[2] = loss_buf[1] + lossr_buf[1]
        lossr_buf[4 + y] = loss_buf[2]
        kept["ly"] = Group(lossr_buf.at[pl.ds(4, 3)])
        for k in (1, 2, 3):
            kept["ly"].send(loss_buf.at[2], lossr_buf.at[4 + y], at_y(k))

    def loss_4():
        kept["ly"].wait_recv()
        loss_buf[3] = lossr_buf[4] + lossr_buf[5] + lossr_buf[6] + lossr_buf[7]
        lossr_buf[8 + z] = loss_buf[3]
        kept["lz"] = Group(lossr_buf.at[pl.ds(8, 3)])
        for k in (1, 2, 3):
            kept["lz"].send(loss_buf.at[3], lossr_buf.at[8 + z], at_z(k))

    def loss_5():
        kept["lz"].wait_recv()
        loss_buf[4] = lossr_buf[8] + lossr_buf[9] + lossr_buf[10] + lossr_buf[11]
        kept["lo"] = remote(loss_buf.at[4], lossr_buf.at[2], x_outer)

    by_chunk = {
        "A": stage_a,
        "B": stage_b,
        "C": stage_c,
        "D": stage_d,
        "E": stage_e,
        "F": stage_f,
        "G": stage_g,
        "H": stage_h,
        "X": gather_x1,
        "Y": gather_x2,
        "Q": hidden_half,
        "R": lambda h: hr[h].wait_recv(),
    }
    once = {
        "N1": rows_second,
        "N2": rows_near,
        "N3": rows_far,
        "N4": nd_side.wait_recv,
        "S1": stat_1,
        "S2": stat_2,
        "S3": stat_3,
        "S4": stat_4,
        "S5": scales,
        "L1": loss_1,
        "L2": loss_2,
        "L3": loss_3,
        "L4": loss_4,
        "L5": loss_5,
    }
    for step in SCHEDULE:
        if step in once:
            once[step]()
        else:
            by_chunk[step[0]](int(step[1]))

    for group in list(open_sends):
        group.wait_send()
    for pair in w_swap + final:
        crossed_sent(pair)
    kept["lo"].wait_recv()
    out_loss[...] = (loss_buf[4] + lossr_buf[2])[0:1, 0:8]

    for jj in range(2):
        for r in range(2):
            got = fr_buf.at[jj, r]
            pltpu.make_async_copy(got, got, cross_sem.at[2 + 2 * jj + r]).wait()
            out_grad[pl.ds(r * 256, 256), pl.ds(jj * 128, 128)] = fr_buf[jj, r].astype(F32).T
    assert used[0] <= SEMS, used[0]


def shards(
    teacher_hidden,
    teacher_gain,
    target_proj,
    student_in,
    student_gain,
    proj_weight,
    doc_ids,
    stream_ids,
    stream_weight,
):
    hbm = pl.BlockSpec(memory_space=pl.ANY)
    vmem = pl.BlockSpec(memory_space=pltpu.VMEM)
    scratch = [
        ((2, 8, 256, 1024), BF),
        ((2, NC, 8, 128, 512), BF),
        ((SLOTS, 8, 256, 512), BF),
        ((NC, 2, 256, 512), BF),
        ((NC, 2, 2, 256, 512), BF),
        ((NC, 256, 512), BF),
        ((NC, 256, 512), BF),
        ((4, 2, 128, D), BF),
        ((4, 4, 256, 512), BF),
        ((2, 4, 256, 256), BF),
        ((2, 4, 256, 256), BF),
        ((2, 128, D), BF),
        ((NC, 4, 256, 128), BF),
        ((NC, 4, 256, 128), BF),
        ((128, 1024), BF),
        ((NC, 2, 128, 512), BF),
        ((NC, 2, 2, 128, 512), BF),
        ((NC, 4, 128, 256), BF),
        ((NC, 4, 128, 256), BF),
        ((NC, 128, 256), BF),
        ((2, 2, 128, 256), BF),
        ((2, 128, 128), F32),
        ((16, 8, 128), F32),
        ((4, 24, 128), F32),
        ((2, 24, 128), F32),
        ((4, 24, 128), F32),
        ((4, 8, 128), F32),
        ((2, 8, 128), F32),
        ((5, 8, 128), F32),
        ((12, 8, 128), F32),
        ((256, 128), F32),
        ((256, 128), F32),
        ((256, 128), F32),
        ((256, 128), F32),
        ((2, 256, 512), F32),
    ]
    w_grad, loss = pl.pallas_call(
        kernel,
        out_shape=(
            jax.ShapeDtypeStruct((512, 256), F32),
            jax.ShapeDtypeStruct((1, 8), F32),
        ),
        in_specs=[hbm, vmem, hbm, hbm, vmem, hbm, vmem, vmem, pl.BlockSpec(memory_space=pltpu.SMEM)],
        out_specs=(vmem, vmem),
        scratch_shapes=[pltpu.VMEM(shape, kind) for shape, kind in scratch]
        + [pltpu.SemaphoreType.DMA((SEMS,)), pltpu.SemaphoreType.DMA((6,))],
        compiler_params=pltpu.CompilerParams(
            collective_id=0, has_side_effects=True, vmem_limit_bytes=62 * 2**20
        ),
        cost_estimate=pl.CostEstimate(flops=26 * 10**9, bytes_accessed=16 * 2**20, transcendentals=0),
    )(
        teacher_hidden.reshape(8, 256, 1024),
        teacher_gain.reshape(8, 128),
        target_proj.reshape(8, 128, D),
        student_in,
        student_gain.reshape(D // 128, 128),
        proj_weight,
        doc_ids.reshape(1, 128),
        stream_ids.reshape(1, 128),
        stream_weight,
    )
    return loss.reshape(8), w_grad


def solution(mesh):
    in_specs = (
        P("seq", "tp"),
        P("tp"),
        P("tp", None),
        P(("seq", "tp"), None),
        P(),
        P("seq", "tp"),
        P(("seq", "tp")),
        P(("seq", "tp")),
        P(),
    )
    out_specs = (P(), P("seq", "tp"))
    return jax.shard_map(shards, mesh=mesh, in_specs=in_specs, out_specs=out_specs, check_vma=False)
```
